32 devices in a mesh: groups: 2 (over y), expert: 4 (over z), dp: 4 (over x, core).
Axes of the slice: x: 2, y: 2, z: 4, core: 2. Of those that a mesh axis runs over, the one named last changes fastest.
Arguments:
- tokens: bfloat16 [2048, 7168], P(('groups', 'expert'), 'dp'), parts along dimension 0, may hold values from -6 to 6
- cotangent: bfloat16 [2048, 7168], P(('groups', 'expert'), 'dp'), parts along dimension 0, may hold values from -6 to 6
- expert_ids: int32 [2048, 8], P(('groups', 'expert')), parts along dimension 0, may hold values from 0 to 255, as said below
- gate_values: bfloat16 [2048, 8], P(('groups', 'expert')), parts along dimension 0, may hold values from 0.049804688 to 1
- w_gate: bfloat16 [7168, 8192], P('dp', 'expert'), may hold values from -0.0625 to 0.0625
- w_up: bfloat16 [7168, 8192], P('dp', 'expert'), may hold values from -0.0625 to 0.0625
- w_down: bfloat16 [7168, 8192], P('dp', 'expert'), may hold values from -0.125 to 0.125
Outputs:
- output: bfloat16 [2048, 7168], P(('groups', 'expert'), 'dp'), parts along dimension 0
- input_grad: bfloat16 [2048, 7168], P(('groups', 'expert'), 'dp'), parts along dimension 0
- gate_grad: bfloat16 [2048, 8], P(('groups', 'expert')), parts along dimension 0
- grad_gate: bfloat16 [14336, 8192], P(('groups', 'dp'), 'expert'), parts along dimension 0
- grad_up: bfloat16 [14336, 8192], P(('groups', 'dp'), 'expert'), parts along dimension 0
- grad_down: bfloat16 [14336, 8192], P(('groups', 'dp'), 'expert'), parts along dimension 0
The draws below stay inside these ranges and needn't reach their ends.
There are 2 independent parts, one for each index of `groups`. The reference program is written for one: setup_inputs(seed, part) draws one part's arguments, and reference() takes and returns one part's arrays. A program takes and returns all parts, laid end to end along the dimension named above; an argument that names none is the same for every part. Nothing has to cross between parts.
Inputs may be any that keep to these rules, and one draw needn't show every extreme that they name: `expert_ids`: each row names 8 different experts. Of the experts 0 to 3, each is named by 1 to 24 of the rows of one aligned block of 256 rows; in every draw one of them is named by exactly 24 rows in every block.
All inputs are finite; a program needn't handle non-finite values.
Results may differ from the reference program's by a relative error of at most 0.0063.
Values may be sent and summed in bfloat16 or wider, within the bound.
No kernel may reach another device: no remote copies, remote signals or barrier semaphores. Data moves between devices by JAX's collectives and lax.ppermute only.
A program may use at most 192 MiB of HBM per device.

```python
import math
import jax
import jax.numpy as jnp
from jax import lax

D = 7168
FF = 2048
EXP_ALL = 256
TOP = 8
EXPERTS = 4
CAP = 24
TOK = 256
TOKENS = 1024
N_EXPERT = 4


def draw_expert_ids(key, part):
    key = jax.random.fold_in(key, 11)
    blocks = TOKENS // TOK
    keys = jax.random.split(key, 6)
    counts = jax.random.randint(keys[0], (blocks, EXPERTS), 1, CAP + 1)
    expert_pick = jax.random.randint(keys[2], (), 0, EXPERTS)
    full = jnp.arange(EXPERTS)[None, :] == expert_pick
    counts = jnp.where(full, CAP, counts)
    scores = jax.random.randint(keys[3], (blocks, TOK, EXPERTS), 0, 1 << 20) * TOK + jnp.arange(TOK)[None, :, None]
    rank = jnp.argsort(jnp.argsort(scores, axis=1), axis=1)
    member = (rank < counts[:, None, :]).reshape(TOKENS, EXPERTS)
    rest = EXP_ALL - EXPERTS
    other_scores = jax.random.randint(keys[4], (TOKENS, rest), 0, 1 << 20) * rest + jnp.arange(rest)[None, :]
    others = jnp.argsort(other_scores, axis=1)[:, :TOP] + EXPERTS
    first = jnp.where(member, jnp.arange(EXPERTS)[None, :], others[:, :EXPERTS])
    ids = jnp.concatenate([first, others[:, EXPERTS:]], axis=1)
    order_scores = jax.random.randint(keys[5], (TOKENS, TOP), 0, 1 << 20) * TOP + jnp.arange(TOP)[None, :]
    order = jnp.argsort(order_scores, axis=1)
    return jnp.take_along_axis(ids, order, axis=1).astype(jnp.int32)


def block_scale(rng, dims, cuts, smallest, top_value):
    gain, own = 1.0, jax.random.fold_in(rng, 6)
    for axis_at, blocks in cuts:
        steps = jnp.exp(jax.random.uniform(jax.random.fold_in(own, axis_at), (blocks,), jnp.float32, smallest / len(cuts), top_value / len(cuts)))
        gain = gain * jnp.repeat(steps, dims[axis_at] // blocks).reshape([-1 if axis == axis_at else 1 for axis in range(len(dims))])
    return gain


def bell_draw(stream_key, dims, width, most, cuts=(), held_as=jnp.bfloat16):
    array = width * jax.random.normal(stream_key, dims, jnp.float32)
    if cuts:
        array = array * block_scale(stream_key, dims, cuts, -0.22, 0.18)
    return jnp.clip(array, -most, most).astype(held_as)


def setup_inputs(seed: int = 0, part: int = 0) -> dict:
    key_list = jax.random.split(jax.random.key(seed), 8)
    part_splits = jax.random.split(jax.random.fold_in(key_list[7], part), 8)
    tokens = bell_draw(part_splits[0], (TOKENS, D), 1.0, 6.0, ((0, 4), (1, 4)))
    cotangent = bell_draw(part_splits[1], (TOKENS, D), 1.0, 6.0, ((0, 4), (1, 4)))
    expert_ids = draw_expert_ids(jax.random.fold_in(jax.random.fold_in(key_list[7], part), 71), part)
    gate_values = jnp.clip(jnp.exp(math.log(1.0) - 2.9996462 * jax.random.uniform(part_splits[3], (TOKENS, TOP), jnp.float32) ** block_scale(part_splits[3], (TOKENS, TOP), ((0, 4),), -0.2, 0.2)), 0.049804688, 1.0).astype(jnp.bfloat16)
    w_gate = bell_draw(key_list[4], (D, EXPERTS * FF), D ** -0.5, 0.0625, ((0, 4), (1, 4)))
    w_up = bell_draw(key_list[5], (D, EXPERTS * FF), D ** -0.5, 0.0625, ((0, 4), (1, 4)))
    w_down = bell_draw(key_list[6], (D, EXPERTS * FF), FF ** -0.5, 0.125, ((0, 4), (1, 4)))
    return dict(tokens=tokens, cotangent=cotangent, expert_ids=expert_ids, gate_values=gate_values, w_gate=w_gate, w_up=w_up, w_down=w_down)


def slot_table(expert_ids, experts, capacity):
    count = expert_ids.shape[0]
    labels = jnp.arange(experts, dtype=jnp.int32)
    member = jnp.any(expert_ids[:, :, None] == labels[None, None, :], axis=1).astype(jnp.int32)
    slot = (jnp.cumsum(member, axis=0) - member).astype(jnp.int32)
    places = jnp.arange(capacity, dtype=jnp.int32)
    chosen = member[:, :, None] * (slot[:, :, None] == places[None, None, :]).astype(jnp.int32)
    position = jnp.arange(count, dtype=jnp.int32)[:, None, None]
    filled = jnp.sum(chosen, axis=0).astype(jnp.int32)
    index = (jnp.sum(chosen * position, axis=0).astype(jnp.int32) + count * (1 - filled)).astype(jnp.int32)
    return member, slot, index


def expert_weights(expert_ids, gate_values, experts):
    labels = jnp.arange(experts, dtype=jnp.int32)
    match = expert_ids[:, :, None] == labels[None, None, :]
    return jnp.sum(jnp.where(match, gate_values.astype(jnp.float32)[:, :, None], jnp.float32(0.0)), axis=1)


def swiglu_grads(hidden_grad, gate, up):
    sigma = jax.nn.sigmoid(gate)
    active = gate * sigma
    d_up = (hidden_grad * active).astype(jnp.bfloat16)
    d_gate = (hidden_grad * up * sigma * (1.0 + gate * (1.0 - sigma))).astype(jnp.bfloat16)
    return d_gate, d_up


def reference(tokens, cotangent, expert_ids, gate_values, w_gate, w_up, w_down):
    blocks = TOKENS // TOK
    span = N_EXPERT // EXPERTS
    slice_width = FF // span
    ids = expert_ids.reshape(blocks, TOK, TOP)
    member, slot, index = jax.vmap(lambda block_ids: slot_table(block_ids, EXPERTS, CAP))(ids)
    weight = jax.vmap(lambda a, b: expert_weights(a, b, EXPERTS))(ids, gate_values.reshape(blocks, TOK, TOP))
    padded_x = jnp.concatenate([tokens.reshape(blocks, TOK, D), jnp.zeros((blocks, 1, D), tokens.dtype)], axis=1)
    dy_blocks = cotangent.reshape(blocks, TOK, D)
    padded_dy = jnp.concatenate([dy_blocks, jnp.zeros((blocks, 1, D), cotangent.dtype)], axis=1)
    padded_w = jnp.concatenate([weight, jnp.zeros((blocks, 1, EXPERTS), jnp.float32)], axis=1)
    take_rows = jax.vmap(lambda a, i: a[i])
    x_rows = take_rows(padded_x, index)
    dy_rows = take_rows(padded_dy, index)
    slot_weight = jax.vmap(lambda w, i: jnp.take_along_axis(w, i.T, axis=0).T)(padded_w, index)
    grad_rows = (slot_weight[..., None] * dy_rows.astype(jnp.float32)).astype(jnp.bfloat16)
    pick = jnp.where(member > 0, slot, CAP).astype(jnp.int32)
    dy_float = dy_blocks.astype(jnp.float32)
    output = jnp.zeros((blocks, TOK, D), jnp.float32)
    input_grad = jnp.zeros((blocks, TOK, D), jnp.float32)
    scores = []
    grads_gate, grads_up, grads_down = [], [], []
    for expert in range(EXPERTS):
        rows = x_rows[:, expert].reshape(-1, D)
        grads = grad_rows[:, expert].reshape(-1, D)

        def stack(w):
            return w[:, expert * FF:(expert + 1) * FF].reshape(D, span, slice_width).transpose(1, 0, 2)

        def one_slice(carry, pieces):
            out_sum, in_sum = carry
            wg, wu, wd = pieces
            gate = jnp.dot(rows, wg, preferred_element_type=jnp.float32)
            up = jnp.dot(rows, wu, preferred_element_type=jnp.float32)
            hidden = (jax.nn.silu(gate) * up).astype(jnp.bfloat16)
            partial_out = jnp.dot(hidden, wd.T, preferred_element_type=jnp.float32).astype(jnp.bfloat16)
            hidden_grad = jnp.dot(grads, wd, preferred_element_type=jnp.float32)
            d_gate, d_up = swiglu_grads(hidden_grad, gate, up)
            part_in = (jnp.dot(d_gate, wg.T, preferred_element_type=jnp.float32)
                       + jnp.dot(d_up, wu.T, preferred_element_type=jnp.float32)).astype(jnp.bfloat16)
            out_sum = out_sum + partial_out.astype(jnp.float32)
            in_sum = in_sum + part_in.astype(jnp.float32)
            dwg = jnp.dot(rows.T, d_gate, preferred_element_type=jnp.float32).astype(jnp.bfloat16)
            dwu = jnp.dot(rows.T, d_up, preferred_element_type=jnp.float32).astype(jnp.bfloat16)
            dwd = jnp.dot(grads.T, hidden, preferred_element_type=jnp.float32).astype(jnp.bfloat16)
            return (out_sum, in_sum), (dwg, dwu, dwd)

        zeros = jnp.zeros((rows.shape[0], D), jnp.float32)
        (out_sum, in_sum), (dwg, dwu, dwd) = lax.scan(one_slice, (zeros, zeros), (stack(w_gate), stack(w_up), stack(w_down)))
        grads_gate.append(dwg.transpose(1, 0, 2).reshape(D, FF))
        grads_up.append(dwu.transpose(1, 0, 2).reshape(D, FF))
        grads_down.append(dwd.transpose(1, 0, 2).reshape(D, FF))
        pad_rows = jnp.zeros((blocks, 1, D), jnp.float32)
        padded_out = jnp.concatenate([out_sum.reshape(blocks, CAP, D), pad_rows], axis=1)
        padded_in = jnp.concatenate([in_sum.reshape(blocks, CAP, D), pad_rows], axis=1)
        picked_out = take_rows(padded_out, pick[:, :, expert])
        picked_in = take_rows(padded_in, pick[:, :, expert])
        output = output + weight[:, :, expert, None] * picked_out
        input_grad = input_grad + picked_in
        scores.append(jnp.sum(dy_float * picked_out, axis=2))
    score_table = jnp.stack(scores, axis=2)
    labels = jnp.arange(EXPERTS, dtype=jnp.int32)
    match = ids[:, :, :, None] == labels[None, None, None, :]
    gate_grad = jnp.sum(jnp.where(match, score_table[:, :, None, :], jnp.float32(0.0)), axis=3)
    return (output.reshape(TOKENS, D).astype(jnp.bfloat16),
            input_grad.reshape(TOKENS, D).astype(jnp.bfloat16),
            gate_grad.reshape(TOKENS, TOP).astype(jnp.bfloat16),
            jnp.concatenate(grads_gate, axis=1),
            jnp.concatenate(grads_up, axis=1),
            jnp.concatenate(grads_down, axis=1))
```

```python
import jax
import jax.numpy as jnp
from jax import lax
from jax.sharding import PartitionSpec as P

EXPERTS = 4
CAP = 24
BF = jnp.bfloat16
F32 = jnp.float32


def dot(left, right, dims):
    return lax.dot_general(left, right, (dims, ((), ())), preferred_element_type=F32)


def swap(value, axis, step):
    size = lax.axis_size(axis)
    return lax.ppermute(value, axis, [(i, i ^ step) for i in range(size)])


def exchange(blocks, axis):
    return [blocks[0]] + [swap(blocks[s], axis, s) for s in range(1, len(blocks))]


def halves(value, core):
    half = value.shape[1] // 2
    mine = lax.dynamic_slice_in_dim(value, core * half, half, 1)
    other = lax.dynamic_slice_in_dim(value, (1 - core) * half, half, 1)
    return mine, other


def dp_sum(values, core):
    size = lax.axis_size("dp")
    pairs = [halves(v, core) for v in values]
    got = [swap(other, "dp", 1) for _, other in pairs]
    sums = [mine + g for (mine, _), g in zip(pairs, got)]
    step = 2
    while step < size:
        got = [swap(s.astype(BF), "dp", step) for s in sums]
        sums = [s + g.astype(F32) for s, g in zip(sums, got)]
        step *= 2
    return sums


def join(mine, core):
    other = swap(mine, "dp", 1)
    first = jnp.where(core == 0, mine, other)
    second = jnp.where(core == 0, other, mine)
    return jnp.concatenate([first, second], axis=1)


def per_device(tokens, cotangent, expert_ids, gate_values, w_gate, w_up, w_down):
    devices = lax.axis_size("expert")
    span = devices // EXPERTS
    count, width = tokens.shape
    me = lax.axis_index("expert")
    core = lax.axis_index("dp") % 2
    direct = devices <= 8

    steps = jnp.arange(devices, dtype=jnp.int32)
    labels = ((steps ^ me) if direct else steps) // span
    match = expert_ids.T[None, :, :] == labels[:, None, None]
    member = jnp.any(match, axis=1)
    weight = jnp.sum(jnp.where(match, gate_values.T.astype(F32)[None], 0.0), axis=1)
    earlier = jnp.arange(count)[:, None] < jnp.arange(count)[None, :]
    slot = dot(member.astype(BF), earlier.astype(BF), ((1,), (0,)))
    places = jnp.arange(CAP, dtype=F32)
    chosen = (slot[:, None, :] == places[None, :, None]) & member[:, None, :]
    pick = chosen.astype(BF).reshape(devices * CAP, count)
    pick_w = jnp.where(chosen, weight[:, None, :], 0.0).astype(BF).reshape(devices * CAP, count)

    def move(rows):
        if direct:
            return jnp.concatenate(
                exchange([rows[s * CAP:(s + 1) * CAP] for s in range(devices)], "expert"), axis=0)
        got = lax.all_to_all(rows.reshape(devices, CAP, -1), "expert", split_axis=0, concat_axis=0, tiled=True)
        return got.reshape(devices * CAP, -1)

    rows = move(dot(pick, tokens, ((1,), (0,))).astype(BF))
    grads = move(dot(pick_w, cotangent, ((1,), (0,))).astype(BF))

    gate, up = dp_sum([dot(rows, w_gate, ((1,), (0,))), dot(rows, w_up, ((1,), (0,)))], core)
    sigma = jax.nn.sigmoid(gate)
    active = gate * sigma
    hidden_h = (active * up).astype(BF)
    hidden = join(hidden_h, core)
    back_out = move(dot(hidden, w_down, ((1,), (1,))).astype(BF))

    (hidden_grad,) = dp_sum([dot(grads, w_down, ((1,), (0,)))], core)
    d_up = join((hidden_grad * active).astype(BF), core)
    d_gate = join((hidden_grad * up * sigma * (1.0 + gate * (1.0 - sigma))).astype(BF), core)
    score = jnp.sum(hidden_grad * hidden_h.astype(F32), axis=1, keepdims=True)
    score = score + swap(score, "dp", 1)
    back_in = move((dot(d_gate, w_gate, ((1,), (1,))) + dot(d_up, w_up, ((1,), (1,)))).astype(BF))
    back_score = move(jnp.broadcast_to(score, (score.shape[0], 128)))[:, :1]

    grad_gate = dot(rows, d_gate, ((0,), (0,))).astype(BF)
    grad_up = dot(rows, d_up, ((0,), (0,))).astype(BF)
    grad_down = dot(grads, hidden, ((0,), (0,))).astype(BF)

    output = dot(pick_w, back_out, ((0,), (0,))).astype(BF)
    input_grad = dot(pick, back_in, ((0,), (0,))).astype(BF)

    per_token = jnp.sum(jnp.where(chosen, back_score.reshape(devices, CAP, 1), 0.0), axis=1)
    gate_grad = jnp.sum(
        jnp.where(match, per_token[:, None, :] / gate_values.T.astype(F32)[None], 0.0), axis=0
    ).T.astype(BF)
    return output, input_grad, gate_grad, grad_gate, grad_up, grad_down


def solution(mesh):
    in_specs = (
        P(("groups", "expert"), "dp"),
        P(("groups", "expert"), "dp"),
        P(("groups", "expert"), None),
        P(("groups", "expert"), None),
        P("dp", "expert"),
        P("dp", "expert"),
        P("dp", "expert"),
    )
    out_specs = (
        P(("groups", "expert"), "dp"),
        P(("groups", "expert"), "dp"),
        P(("groups", "expert"), None),
        P(("groups", "dp"), "expert"),
        P(("groups", "dp"), "expert"),
        P(("groups", "dp"), "expert"),
    )
    return jax.shard_map(
        per_device, mesh=mesh, in_specs=in_specs, out_specs=out_specs, check_vma=False
    )
```

```python
import jax
import jax.numpy as jnp
from jax import lax
from jax.experimental import pallas as pl
from jax.experimental.pallas import tpu as pltpu
from jax.sharding import PartitionSpec as P

EXPERTS = 4
CAP = 24
EXTRA = 128
BF = jnp.bfloat16
F32 = jnp.float32


def dot(left, right, dims):
    return lax.dot_general(left, right, (dims, ((), ())), preferred_element_type=F32)


def swap(value, axis, step):
    size = lax.axis_size(axis)
    return lax.ppermute(value, axis, [(i, i ^ step) for i in range(size)])


def exchange(blocks, axis):
    return [blocks[0]] + [swap(blocks[s], axis, s) for s in range(1, len(blocks))]


def dp_sum(values, even):
    size = lax.axis_size("dp")
    half = values[0].shape[1] // 2
    mine = [jnp.where(even, v[:, :half], v[:, half:]) for v in values]
    other = [jnp.where(even, v[:, half:], v[:, :half]) for v in values]
    got = swap(jnp.concatenate(other, axis=1), "dp", 1)
    total = jnp.concatenate(mine, axis=1) + got
    step = 2
    while step < size:
        total = total + swap(total.astype(BF), "dp", step).astype(F32)
        step *= 2
    return [total[:, i * half:(i + 1) * half] for i in range(len(values))]


def join(values, even):
    half = values[0].shape[1]
    other = swap(jnp.concatenate(values, axis=1), "dp", 1)
    out = []
    for i, v in enumerate(values):
        o = other[:, i * half:(i + 1) * half]
        out.append(jnp.concatenate([jnp.where(even, v, o), jnp.where(even, o, v)], axis=1))
    return out


def weight_grads(rows, cots):
    count, width = rows.shape
    hidden = cots[0].shape[1]
    n = len(cots)
    block = width // 7 if width % (7 * 128) == 0 else 128

    def body(rows_ref, *refs):
        cot_refs, outs, buf, sem = refs[:n], refs[n:2 * n], refs[2 * n], refs[2 * n + 1]
        values = [c[...] for c in cot_refs]
        for at in range(0, width, block):
            part = rows_ref[:, at:at + block]
            for i in range(n):
                buf[i, at:at + block, :] = dot(part, values[i], ((0,), (0,))).astype(BF)
                pltpu.make_async_copy(
                    buf.at[i, pl.ds(at, block)], outs[i].at[pl.ds(at, block)], sem.at[i]
                ).start()
        for i in range(n):
            pltpu.make_async_copy(buf.at[i], outs[i], sem.at[i]).wait()

    size = n * width * hidden * 2
    vmem = pl.BlockSpec(memory_space=pltpu.VMEM)
    return pl.pallas_call(
        body,
        in_specs=[vmem] * (n + 1),
        out_specs=[pl.BlockSpec(memory_space=pl.ANY)] * n,
        out_shape=[jax.ShapeDtypeStruct((width, hidden), BF)] * n,
        scratch_shapes=[pltpu.VMEM((n, width, hidden), BF), pltpu.SemaphoreType.DMA((n,))],
        compiler_params=pltpu.CompilerParams(vmem_limit_bytes=size + (8 << 20)),
        cost_estimate=pl.CostEstimate(flops=size * count, bytes_accessed=size, transcendentals=0),
    )(rows, *cots)


def per_device(tokens, cotangent, expert_ids, gate_values, w_gate, w_up, w_down):
    devices = lax.axis_size("expert")
    span = devices // EXPERTS
    count, width = tokens.shape
    direct = devices <= 8
    even = lax.axis_index("dp") % 2 == 0
    me = lax.axis_index("expert")
    expert_ids, even, me = lax.optimization_barrier((expert_ids, even, me))

    steps = jnp.arange(devices, dtype=jnp.int32)
    labels = ((steps ^ me) if direct else steps) // span
    match = expert_ids.T[None, :, :] == labels[:, None, None]
    member = jnp.any(match, axis=1)
    weight = jnp.sum(jnp.where(match, gate_values.T.astype(F32)[None], 0.0), axis=1)
    earlier = jnp.arange(count)[:, None] < jnp.arange(count)[None, :]
    slot = dot(member.astype(BF), earlier.astype(BF), ((1,), (0,)))
    places = jnp.arange(CAP, dtype=F32)
    chosen = (slot[:, None, :] == places[None, :, None]) & member[:, None, :]
    pick = chosen.astype(BF).reshape(devices * CAP, count)
    pick_w = jnp.where(chosen, weight[:, None, :], 0.0).astype(BF).reshape(devices * CAP, count)

    def move(rows):
        if direct:
            return jnp.concatenate(
                exchange([rows[s * CAP:(s + 1) * CAP] for s in range(devices)], "expert"), axis=0)
        got = lax.all_to_all(rows.reshape(devices, CAP, -1), "expert", split_axis=0, concat_axis=0, tiled=True)
        return got.reshape(devices * CAP, -1)

    rows = move(dot(pick, tokens, ((1,), (0,))).astype(BF))
    grads = move(dot(pick_w, cotangent, ((1,), (0,))).astype(BF))

    gate, up = dp_sum([dot(rows, w_gate, ((1,), (0,))), dot(rows, w_up, ((1,), (0,)))], even)
    sigma = jax.nn.sigmoid(gate)
    active = gate * sigma
    hidden_h = (active * up).astype(BF)
    (hidden,) = join([hidden_h], even)
    back_out = move(dot(hidden, w_down, ((1,), (1,))).astype(BF))

    (hidden_grad,) = dp_sum([dot(grads, w_down, ((1,), (0,)))], even)
    d_up, d_gate = join(
        [
            (hidden_grad * active).astype(BF),
            (hidden_grad * up * sigma * (1.0 + gate * (1.0 - sigma))).astype(BF),
        ],
        even,
    )
    score = jnp.sum(hidden_grad * hidden_h.astype(F32), axis=1, keepdims=True)
    score = score + swap(score, "dp", 1)
    high = lax.reduce_precision(score, 8, 7)
    low = (score - high).astype(BF)
    high = high.astype(BF)
    lanes = jnp.arange(EXTRA)[None, :]
    extra = jnp.where(lanes < EXTRA // 2, high, low)
    part_in = (dot(d_gate, w_gate, ((1,), (1,))) + dot(d_up, w_up, ((1,), (1,)))).astype(BF)
    back_in = move(jnp.concatenate([part_in, extra], axis=1))

    late_grads, late_w = lax.optimization_barrier((grads, pick_w, part_in))[:2]
    (grad_down,) = weight_grads(late_grads, [hidden])
    grad_gate, grad_up = weight_grads(rows, [d_gate, d_up])

    output = dot(late_w, back_out, ((0,), (0,))).astype(BF)
    input_grad = dot(pick, back_in[:, :width], ((0,), (0,))).astype(BF)

    source = jnp.arange(devices * CAP)[:, None] // CAP
    placed = jnp.where(source == lanes % (EXTRA // 2), back_in[:, width:], jnp.zeros((), BF))
    per_token = dot(placed, pick, ((0,), (0,)))
    per_token = per_token[:devices] + per_token[EXTRA // 2:EXTRA // 2 + devices]
    gate_grad = jnp.sum(
        jnp.where(match, per_token[:, None, :] / gate_values.T.astype(F32)[None], 0.0), axis=0
    ).T.astype(BF)
    return output, input_grad, gate_grad, grad_gate, grad_up, grad_down


def solution(mesh):
    in_specs = (
        P(("groups", "expert"), "dp"),
        P(("groups", "expert"), "dp"),
        P(("groups", "expert"), None),
        P(("groups", "expert"), None),
        P("dp", "expert"),
        P("dp", "expert"),
        P("dp", "expert"),
    )
    out_specs = (
        P(("groups", "expert"), "dp"),
        P(("groups", "expert"), "dp"),
        P(("groups", "expert"), None),
        P(("groups", "dp"), "expert"),
        P(("groups", "dp"), "expert"),
        P(("groups", "dp"), "expert"),
    )
    return jax.shard_map(
        per_device, mesh=mesh, in_specs=in_specs, out_specs=out_specs, check_vma=False
    )
```

```python
import jax
import jax.numpy as jnp
from jax import lax
from jax.experimental import pallas as pl
from jax.experimental.pallas import tpu as pltpu
from jax.sharding import PartitionSpec as P

EXPERTS = 4
CAP = 24
EXTRA = 128
BF = jnp.bfloat16
F32 = jnp.float32


def dot(left, right, dims):
    return lax.dot_general(left, right, (dims, ((), ())), preferred_element_type=F32)


def swap(value, axis, step):
    size = lax.axis_size(axis)
    return lax.ppermute(value, axis, [(i, i ^ step) for i in range(size)])


def exchange(blocks, axis, last=1):
    size = len(blocks)
    got = {0: blocks[0]}
    for step in sorted(range(1, size), key=lambda step: (step == last, step)):
        got[step] = swap(blocks[step], axis, step)
    return [got[step] for step in range(size)]


def held(value):
    return pltpu.with_memory_space_constraint(value, pltpu.VMEM)


def project(rows, weight):
    hidden = weight.shape[1]
    tile = min(512, hidden)

    def body(rows_ref, weight_ref, out_ref):
        values = rows_ref[...]
        for at in range(0, hidden, tile):
            out_ref[:, at:at + tile] = dot(values, weight_ref[:, at:at + tile], ((1,), (0,)))

    vmem = pl.BlockSpec(memory_space=pltpu.VMEM)
    flops = 2 * rows.shape[0] * weight.shape[0] * hidden
    return pl.pallas_call(
        body,
        in_specs=[vmem, vmem],
        out_specs=vmem,
        out_shape=jax.ShapeDtypeStruct((rows.shape[0], hidden), F32),
        compiler_params=pltpu.CompilerParams(vmem_limit_bytes=5 << 20),
        cost_estimate=pl.CostEstimate(flops=flops, bytes_accessed=1 << 20, transcendentals=0),
    )(rows, held(weight))


def split_rows(packed, refs):
    if len(refs) == 1:
        refs[0][...] = packed.astype(BF)
        return
    for s, ref in enumerate(refs):
        ref[...] = packed[s * CAP:(s + 1) * CAP].astype(BF)


def pack_shapes(blocks, split, width):
    if split:
        return [jax.ShapeDtypeStruct((CAP, width), BF)] * blocks
    return [jax.ShapeDtypeStruct((blocks * CAP, width), BF)]


def in_hbm(value):
    return pltpu.with_memory_space_constraint(value, pltpu.HBM)


def route(labels, ids, gates, tokens, blocks, split):
    count = ids.shape[1]
    total = blocks * CAP
    pad = max(8, blocks)
    packs = pack_shapes(blocks, split, tokens.shape[1])

    def body(labels_ref, ids_hbm, gates_hbm, tokens_hbm, pick_ref, pick_w_ref, *refs):
        outs, (ids_ref, gates_ref, tokens_ref, sem) = refs[:-4], refs[-4:]
        copies = [
            pltpu.make_async_copy(src, dst, sem.at[i])
            for i, (src, dst) in enumerate(
                ((ids_hbm, ids_ref), (gates_hbm, gates_ref), (tokens_hbm, tokens_ref)))
        ]
        for copy in copies:
            copy.start()
        copies[0].wait()
        copies[1].wait()
        ids_v = ids_ref[...]
        gates_v = gates_ref[...].astype(F32)
        row = lax.broadcasted_iota(jnp.int32, (pad, count), 0)
        member = jnp.zeros((pad, count), F32)
        found, weights = [], []
        for s in range(blocks):
            match = ids_v == labels_ref[s]
            found.append(jnp.max(jnp.where(match, 1.0, 0.0), axis=0, keepdims=True))
            weights.append(jnp.sum(jnp.where(match, gates_v, 0.0), axis=0, keepdims=True))
            member = jnp.where(row == s, found[s], member)
        left = lax.broadcasted_iota(jnp.int32, (count, count), 0)
        right = lax.broadcasted_iota(jnp.int32, (count, count), 1)
        earlier = jnp.where(left < right, 1.0, 0.0).astype(BF)
        slot = dot(member.astype(BF), earlier, ((1,), (0,)))
        place = lax.broadcasted_iota(jnp.int32, (CAP, count), 0).astype(F32)
        plain, weighted = [], []
        for s in range(blocks):
            chosen = jnp.where(slot[s:s + 1] == place, found[s], 0.0)
            plain.append(chosen)
            weighted.append(chosen * weights[s])
        pick = jnp.concatenate(plain, axis=0).astype(BF)
        pick_ref[...] = pick
        pick_w_ref[...] = jnp.concatenate(weighted, axis=0).astype(BF)
        copies[2].wait()
        split_rows(dot(pick, tokens_ref[...], ((1,), (0,))), outs)

    vmem = pl.BlockSpec(memory_space=pltpu.VMEM)
    hbm = pl.BlockSpec(memory_space=pltpu.HBM)
    out = pl.pallas_call(
        body,
        in_specs=[pl.BlockSpec(memory_space=pltpu.SMEM)] + [hbm] * 3,
        out_specs=[vmem] * (2 + len(packs)),
        out_shape=[jax.ShapeDtypeStruct((total, count), BF)] * 2 + packs,
        scratch_shapes=[
            pltpu.VMEM(ids.shape, ids.dtype),
            pltpu.VMEM(gates.shape, gates.dtype),
            pltpu.VMEM(tokens.shape, tokens.dtype),
            pltpu.SemaphoreType.DMA((3,)),
        ],
        compiler_params=pltpu.CompilerParams(vmem_limit_bytes=10 << 20),
        cost_estimate=pl.CostEstimate(flops=1 << 34, bytes_accessed=1 << 20, transcendentals=0),
    )(labels, in_hbm(ids), in_hbm(gates), in_hbm(tokens))
    return out[0], out[1], list(out[2:])


def pack_cotangent(pick_w, cotangent, after, blocks, split):
    packs = pack_shapes(blocks, split, cotangent.shape[1])

    def body(pick_ref, cot_ref, after_ref, *outs):
        split_rows(dot(pick_ref[...], cot_ref[...], ((1,), (0,))), outs)

    vmem = pl.BlockSpec(memory_space=pltpu.VMEM)
    out = pl.pallas_call(
        body,
        in_specs=[vmem, vmem, pl.BlockSpec(memory_space=pl.ANY)],
        out_specs=[vmem] * len(packs),
        out_shape=packs,
        compiler_params=pltpu.CompilerParams(vmem_limit_bytes=8 << 20),
        cost_estimate=pl.CostEstimate(flops=1 << 20, bytes_accessed=1 << 10, transcendentals=0),
    )(pick_w, cotangent, after)
    return list(out)


def send_columns(mat, values, buf, out, sem, width):
    block = width // 2 if width % 256 == 0 else width
    for at in range(0, width, block):
        buf[:, at:at + block] = dot(mat, values[:, at:at + block], ((0,), (0,))).astype(BF)
        pltpu.make_async_copy(buf.at[:, pl.ds(at, block)], out.at[:, pl.ds(at, block)], sem).start()


def finish(labels, ids, gates, pick, back):
    total, count = pick.shape
    blocks = total // CAP
    width = back.shape[1] - EXTRA

    def body(labels_ref, ids_ref, gates_ref, pick_ref, back_ref, out, gate_grad_ref, buf, sem):
        mat = pick_ref[...]
        send_columns(mat, back_ref, buf, out, sem, width)
        source = lax.broadcasted_iota(jnp.int32, (total, EXTRA), 0) // CAP
        lane = lax.broadcasted_iota(jnp.int32, (total, EXTRA), 1) % (EXTRA // 2)
        extra = back_ref[:, width:].astype(F32)
        placed = jnp.where(source == lane, extra, 0.0).astype(BF)
        score = dot(placed, mat, ((0,), (0,)))
        score = score[:EXTRA // 2] + score[EXTRA // 2:]
        ids_v = ids_ref[...]
        grad = jnp.zeros(ids_v.shape, F32)
        for s in range(blocks):
            grad = grad + jnp.where(ids_v == labels_ref[s], score[s:s + 1], 0.0)
        gate_grad_ref[...] = (grad / gates_ref[...].astype(F32)).astype(BF)
        pltpu.make_async_copy(buf, out, sem).wait()

    vmem = pl.BlockSpec(memory_space=pltpu.VMEM)
    return pl.pallas_call(
        body,
        in_specs=[pl.BlockSpec(memory_space=pltpu.SMEM)] + [vmem] * 4,
        out_specs=[pl.BlockSpec(memory_space=pl.ANY), vmem],
        out_shape=[jax.ShapeDtypeStruct((count, width), BF), jax.ShapeDtypeStruct(ids.shape, BF)],
        scratch_shapes=[pltpu.VMEM((count, width), BF), pltpu.SemaphoreType.DMA],
        compiler_params=pltpu.CompilerParams(vmem_limit_bytes=10 << 20),
        cost_estimate=pl.CostEstimate(flops=1 << 20, bytes_accessed=1 << 20, transcendentals=0),
    )(labels, ids, gates, pick, back)


def core_sum(value, even):
    half = value.shape[1] // 2
    mine = jnp.where(even, value[:, :half], value[:, half:])
    other = jnp.where(even, value[:, half:], value[:, :half])
    return mine + swap(other, "dp", 1)


def first_swap(total):
    return swap(total.astype(BF), "dp", 2)


def chip_sum(total, got):
    total = total + got.astype(F32)
    step = 4
    while step < lax.axis_size("dp"):
        total = total + swap(total.astype(BF), "dp", step).astype(F32)
        step *= 2
    return total


def join(values, even):
    half = values[0].shape[1]
    other = swap(jnp.concatenate(values, axis=1), "dp", 1)
    out = []
    for i, v in enumerate(values):
        o = other[:, i * half:(i + 1) * half]
        out.append(jnp.concatenate([jnp.where(even, v, o), jnp.where(even, o, v)], axis=1))
    return out


def weight_grads(rows, cots, pick_w=None, back=None):
    count, width = rows.shape
    hidden = cots[0].shape[1]
    n = len(cots)
    block = 256 if width % 256 == 0 else 128
    combine = pick_w is not None

    def body(*refs):
        rows_ref, cot_refs, refs = refs[0], refs[1:1 + n], refs[1 + n:]
        if combine:
            pick_ref, back_ref, refs = refs[0], refs[1], refs[2:]
        outs, bufs, sem = refs[:n + combine], refs[n + combine:-1], refs[-1]
        if combine:
            send_columns(pick_ref[...], back_ref, bufs[n], outs[n], sem.at[n], width)
        values = [c[...] for c in cot_refs]
        for at in range(0, width, block):
            part = rows_ref[:, at:at + block]
            for i in range(n):
                bufs[i][at:at + block, :] = dot(part, values[i], ((0,), (0,))).astype(BF)
                pltpu.make_async_copy(
                    bufs[i].at[pl.ds(at, block)], outs[i].at[pl.ds(at, block)], sem.at[i]
                ).start()
        for i in range(n + combine):
            pltpu.make_async_copy(bufs[i], outs[i], sem.at[i]).wait()

    shapes = [(width, hidden)] * n + ([(pick_w.shape[1], width)] if combine else [])
    size = n * width * hidden * 2
    vmem = pl.BlockSpec(memory_space=pltpu.VMEM)
    operands = [rows, *cots] + ([pick_w, back] if combine else [])
    return pl.pallas_call(
        body,
        in_specs=[vmem] * len(operands),
        out_specs=[pl.BlockSpec(memory_space=pl.ANY)] * len(shapes),
        out_shape=[jax.ShapeDtypeStruct(shape, BF) for shape in shapes],
        scratch_shapes=[pltpu.VMEM(shape, BF) for shape in shapes]
        + [pltpu.SemaphoreType.DMA((len(shapes),))],
        compiler_params=pltpu.CompilerParams(vmem_limit_bytes=size + (10 << 20)),
        cost_estimate=pl.CostEstimate(flops=size * count, bytes_accessed=size, transcendentals=0),
    )(*operands)


def per_device(tokens, cotangent, expert_ids, gate_values, w_gate, w_up, w_down):
    devices = lax.axis_size("expert")
    span = devices // EXPERTS
    count, width = tokens.shape
    direct = devices <= 8
    even = lax.axis_index("dp") % 2 == 0
    me = lax.axis_index("expert")
    expert_ids, even, me = lax.optimization_barrier((expert_ids, even, me))

    steps = jnp.arange(devices, dtype=jnp.int32)
    labels = ((steps ^ me) if direct else steps) // span
    ids, gates = expert_ids.T, gate_values.T
    pick, pick_w, packed_x = route(labels, ids, gates, tokens, devices, direct)

    def move(blocks):
        if direct:
            return jnp.concatenate(exchange(blocks, "expert"), axis=0)
        rows = jnp.concatenate(blocks, axis=0) if len(blocks) > 1 else blocks[0]
        got = lax.all_to_all(rows.reshape(devices, CAP, -1), "expert", split_axis=0, concat_axis=0, tiled=True)
        return got.reshape(devices * CAP, -1)

    def cut(rows):
        return [rows[s * CAP:(s + 1) * CAP] for s in range(devices)] if direct else [rows]

    if direct:
        got = exchange(packed_x, "expert")
        rows = jnp.concatenate(got, axis=0)
    else:
        rows = move(packed_x)
    gate = core_sum(project(rows, w_gate), even)
    up = core_sum(project(rows, w_up), even)
    gate_swap, up_swap = first_swap(gate), first_swap(up)
    packed_g = pack_cotangent(pick_w, cotangent, up, devices, direct)
    packed_g = exchange(packed_g, "expert") if direct else [move(packed_g)]
    grads = jnp.concatenate(packed_g, axis=0)
    gate, up, grads = lax.optimization_barrier((gate, up, grads))
    hidden_grad = core_sum(project(grads, w_down), even)
    grad_swap = first_swap(hidden_grad)
    gate = chip_sum(gate, gate_swap)
    up = chip_sum(up, up_swap)
    sigma = jax.nn.sigmoid(gate)
    active = gate * sigma
    hidden_h, gate, up, sigma, active, hidden_grad = lax.optimization_barrier(
        ((active * up).astype(BF), gate, up, sigma, active, hidden_grad))
    (hidden,) = join([hidden_h], even)
    part_out = dot(hidden, w_down, ((1,), (1,))).astype(BF)
    hidden_grad = chip_sum(hidden_grad, grad_swap)
    d_up = (hidden_grad * active).astype(BF)
    d_gate = (hidden_grad * up * sigma * (1.0 + gate * (1.0 - sigma))).astype(BF)
    (grad_down,) = weight_grads(grads, [hidden])
    part_out, d_up, d_gate, grad_down = lax.optimization_barrier((part_out, d_up, d_gate, grad_down))
    back_out = exchange(cut(part_out), "expert") if direct else [move(cut(part_out))]
    d_up, d_gate = join([d_up, d_gate], even)
    score = jnp.sum(hidden_grad * hidden_h.astype(F32), axis=1, keepdims=True)
    score = score + swap(score, "dp", 1)
    step = 2
    while step < lax.axis_size("dp"):
        score = 0.5 * (score + swap(score, "dp", step))
        step *= 2
    high = lax.reduce_precision(score, 8, 7)
    low = (score - high).astype(BF)
    high = high.astype(BF)
    lanes = jnp.arange(EXTRA)[None, :]
    extra = jnp.where(lanes < EXTRA // 2, high, low)
    part_in = (dot(d_gate, w_gate, ((1,), (1,))) + dot(d_up, w_up, ((1,), (1,)))).astype(BF)
    back_in = move(cut(jnp.concatenate([part_in, extra], axis=1)))

    late_w, back_out[0] = lax.optimization_barrier((pick_w, back_out[0], part_in))[:2]
    back_out = jnp.concatenate(back_out, axis=0)
    grad_gate, grad_up, output = weight_grads(rows, [d_gate, d_up], late_w, back_out)
    input_grad, gate_grad = finish(labels, ids, gates, pick, back_in)
    return output, input_grad, gate_grad.T, grad_gate, grad_up, grad_down


def solution(mesh):
    in_specs = (
        P(("groups", "expert"), "dp"),
        P(("groups", "expert"), "dp"),
        P(("groups", "expert"), None),
        P(("groups", "expert"), None),
        P("dp", "expert"),
        P("dp", "expert"),
        P("dp", "expert"),
    )
    out_specs = (
        P(("groups", "expert"), "dp"),
        P(("groups", "expert"), "dp"),
        P(("groups", "expert"), None),
        P(("groups", "dp"), "expert"),
        P(("groups", "dp"), "expert"),
        P(("groups", "dp"), "expert"),
    )
    return jax.shard_map(
        per_device, mesh=mesh, in_specs=in_specs, out_specs=out_specs, check_vma=False
    )
```

```python
import jax
import jax.numpy as jnp
from jax import lax
from jax.experimental import pallas as pl
from jax.experimental.pallas import tpu as pltpu
from jax.sharding import PartitionSpec as P

EXPERTS = 4
CAP = 24
EXTRA = 128
BF = jnp.bfloat16
F32 = jnp.float32


def dot(left, right, dims):
    return lax.dot_general(left, right, (dims, ((), ())), preferred_element_type=F32)


def swap(value, axis, step):
    size = lax.axis_size(axis)
    return lax.ppermute(value, axis, [(i, i ^ step) for i in range(size)])


def exchange(blocks, axis, last=1):
    size = len(blocks)
    got = {0: blocks[0]}
    for step in sorted(range(1, size), key=lambda step: (step == last, step)):
        got[step] = swap(blocks[step], axis, step)
    return [got[step] for step in range(size)]


def held(value):
    return pltpu.with_memory_space_constraint(value, pltpu.VMEM)


def project(rows, weight):
    hidden = weight.shape[1]
    tile = min(512, hidden)

    def body(rows_ref, weight_ref, out_ref):
        values = rows_ref[...]
        for at in range(0, hidden, tile):
            out_ref[:, at:at + tile] = dot(values, weight_ref[:, at:at + tile], ((1,), (0,)))

    vmem = pl.BlockSpec(memory_space=pltpu.VMEM)
    flops = 2 * rows.shape[0] * weight.shape[0] * hidden
    return pl.pallas_call(
        body,
        in_specs=[vmem, vmem],
        out_specs=vmem,
        out_shape=jax.ShapeDtypeStruct((rows.shape[0], hidden), F32),
        compiler_params=pltpu.CompilerParams(vmem_limit_bytes=5 << 20),
        cost_estimate=pl.CostEstimate(flops=flops, bytes_accessed=1 << 20, transcendentals=0),
    )(rows, held(weight))


def split_rows(packed, refs):
    if len(refs) == 1:
        refs[0][...] = packed.astype(BF)
        return
    for s, ref in enumerate(refs):
        ref[...] = packed[s * CAP:(s + 1) * CAP].astype(BF)


def pack_shapes(blocks, split, width):
    if split:
        return [jax.ShapeDtypeStruct((CAP, width), BF)] * blocks
    return [jax.ShapeDtypeStruct((blocks * CAP, width), BF)]


def in_hbm(value):
    return pltpu.with_memory_space_constraint(value, pltpu.HBM)


def route(labels, ids, gates, tokens, blocks, split):
    count = ids.shape[1]
    total = blocks * CAP
    pad = max(8, blocks)
    packs = pack_shapes(blocks, split, tokens.shape[1])

    def body(labels_ref, ids_hbm, gates_hbm, tokens_hbm, pick_ref, pick_w_ref, *refs):
        outs, (ids_ref, gates_ref, tokens_ref, sem) = refs[:-4], refs[-4:]
        copies = [
            pltpu.make_async_copy(src, dst, sem.at[i])
            for i, (src, dst) in enumerate(
                ((ids_hbm, ids_ref), (gates_hbm, gates_ref), (tokens_hbm, tokens_ref)))
        ]
        for copy in copies:
            copy.start()
        copies[0].wait()
        copies[1].wait()
        ids_v = ids_ref[...]
        gates_v = gates_ref[...].astype(F32)
        row = lax.broadcasted_iota(jnp.int32, (pad, count), 0)
        member = jnp.zeros((pad, count), F32)
        found, weights = [], []
        for s in range(blocks):
            match = ids_v == labels_ref[s]
            found.append(jnp.max(jnp.where(match, 1.0, 0.0), axis=0, keepdims=True))
            weights.append(jnp.sum(jnp.where(match, gates_v, 0.0), axis=0, keepdims=True))
            member = jnp.where(row == s, found[s], member)
        left = lax.broadcasted_iota(jnp.int32, (count, count), 0)
        right = lax.broadcasted_iota(jnp.int32, (count, count), 1)
        earlier = jnp.where(left < right, 1.0, 0.0).astype(BF)
        slot = dot(member.astype(BF), earlier, ((1,), (0,)))
        place = lax.broadcasted_iota(jnp.int32, (CAP, count), 0).astype(F32)
        plain, weighted = [], []
        for s in range(blocks):
            chosen = jnp.where(slot[s:s + 1] == place, found[s], 0.0)
            plain.append(chosen)
            weighted.append(chosen * weights[s])
        pick = jnp.concatenate(plain, axis=0).astype(BF)
        pick_ref[...] = pick
        pick_w_ref[...] = jnp.concatenate(weighted, axis=0).astype(BF)
        copies[2].wait()
        split_rows(dot(pick, tokens_ref[...], ((1,), (0,))), outs)

    vmem = pl.BlockSpec(memory_space=pltpu.VMEM)
    hbm = pl.BlockSpec(memory_space=pltpu.HBM)
    out = pl.pallas_call(
        body,
        in_specs=[pl.BlockSpec(memory_space=pltpu.SMEM)] + [hbm] * 3,
        out_specs=[vmem] * (2 + len(packs)),
        out_shape=[jax.ShapeDtypeStruct((total, count), BF)] * 2 + packs,
        scratch_shapes=[
            pltpu.VMEM(ids.shape, ids.dtype),
            pltpu.VMEM(gates.shape, gates.dtype),
            pltpu.VMEM(tokens.shape, tokens.dtype),
            pltpu.SemaphoreType.DMA((3,)),
        ],
        compiler_params=pltpu.CompilerParams(vmem_limit_bytes=10 << 20),
        cost_estimate=pl.CostEstimate(flops=1 << 34, bytes_accessed=1 << 20, transcendentals=0),
    )(labels, in_hbm(ids), in_hbm(gates), in_hbm(tokens))
    return out[0], out[1], list(out[2:])


def pack_cotangent(pick_w, cotangent, after, blocks, split):
    packs = pack_shapes(blocks, split, cotangent.shape[1])

    def body(pick_ref, cot_ref, after_ref, *outs):
        split_rows(dot(pick_ref[...], cot_ref[...], ((1,), (0,))), outs)

    vmem = pl.BlockSpec(memory_space=pltpu.VMEM)
    out = pl.pallas_call(
        body,
        in_specs=[vmem, vmem, pl.BlockSpec(memory_space=pl.ANY)],
        out_specs=[vmem] * len(packs),
        out_shape=packs,
        compiler_params=pltpu.CompilerParams(vmem_limit_bytes=8 << 20),
        cost_estimate=pl.CostEstimate(flops=1 << 20, bytes_accessed=1 << 10, transcendentals=0),
    )(pick_w, cotangent, after)
    return list(out)


def send_columns(mat, values, buf, out, sem, width):
    block = width // 2 if width % 256 == 0 else width
    for at in range(0, width, block):
        buf[:, at:at + block] = dot(mat, values[:, at:at + block], ((0,), (0,))).astype(BF)
        pltpu.make_async_copy(buf.at[:, pl.ds(at, block)], out.at[:, pl.ds(at, block)], sem).start()


def finish(labels, ids, gates, pick, back):
    total, count = pick.shape
    blocks = total // CAP
    width = back.shape[1] - EXTRA

    def body(labels_ref, ids_ref, gates_ref, pick_ref, back_ref, out, gate_grad_ref, buf, sem):
        mat = pick_ref[...]
        send_columns(mat, back_ref, buf, out, sem, width)
        source = lax.broadcasted_iota(jnp.int32, (total, EXTRA), 0) // CAP
        lane = lax.broadcasted_iota(jnp.int32, (total, EXTRA), 1) % (EXTRA // 2)
        extra = back_ref[:, width:].astype(F32)
        placed = jnp.where(source == lane, extra, 0.0).astype(BF)
        score = dot(placed, mat, ((0,), (0,)))
        score = score[:EXTRA // 2] + score[EXTRA // 2:]
        ids_v = ids_ref[...]
        grad = jnp.zeros(ids_v.shape, F32)
        for s in range(blocks):
            grad = grad + jnp.where(ids_v == labels_ref[s], score[s:s + 1], 0.0)
        gate_grad_ref[...] = (grad / gates_ref[...].astype(F32)).astype(BF)
        pltpu.make_async_copy(buf, out, sem).wait()

    vmem = pl.BlockSpec(memory_space=pltpu.VMEM)
    return pl.pallas_call(
        body,
        in_specs=[pl.BlockSpec(memory_space=pltpu.SMEM)] + [vmem] * 4,
        out_specs=[pl.BlockSpec(memory_space=pl.ANY), vmem],
        out_shape=[jax.ShapeDtypeStruct((count, width), BF), jax.ShapeDtypeStruct(ids.shape, BF)],
        scratch_shapes=[pltpu.VMEM((count, width), BF), pltpu.SemaphoreType.DMA],
        compiler_params=pltpu.CompilerParams(vmem_limit_bytes=10 << 20),
        cost_estimate=pl.CostEstimate(flops=1 << 20, bytes_accessed=1 << 20, transcendentals=0),
    )(labels, ids, gates, pick, back)


def core_sum(value, even):
    half = value.shape[1] // 2
    mine = jnp.where(even, value[:, :half], value[:, half:])
    other = jnp.where(even, value[:, half:], value[:, :half])
    return mine + swap(other, "dp", 1)


def first_swap(total):
    return swap(total.astype(BF), "dp", 2)


def chip_sum(total, got):
    total = total + got.astype(F32)
    step = 4
    while step < lax.axis_size("dp"):
        total = total + swap(total.astype(BF), "dp", step).astype(F32)
        step *= 2
    return total


def shared_sum(total, got):
    return lax.reduce_precision(total, 8, 7) + got.astype(F32)


def join(values, even):
    half = values[0].shape[1]
    other = swap(jnp.concatenate(values, axis=1), "dp", 1)
    out = []
    for i, v in enumerate(values):
        o = other[:, i * half:(i + 1) * half]
        out.append(jnp.concatenate([jnp.where(even, v, o), jnp.where(even, o, v)], axis=1))
    return out


def weight_grads(rows, cots, pick_w=None, back=None):
    count, width = rows.shape
    hidden = cots[0].shape[1]
    n = len(cots)
    block = 256 if width % 256 == 0 else 128
    combine = pick_w is not None

    def body(*refs):
        rows_ref, cot_refs, refs = refs[0], refs[1:1 + n], refs[1 + n:]
        if combine:
            pick_ref, back_ref, refs = refs[0], refs[1], refs[2:]
        outs, bufs, sem = refs[:n + combine], refs[n + combine:-1], refs[-1]
        if combine:
            send_columns(pick_ref[...], back_ref, bufs[n], outs[n], sem.at[n], width)
        values = [c[...] for c in cot_refs]
        for at in range(0, width, block):
            part = rows_ref[:, at:at + block]
            for i in range(n):
                bufs[i][at:at + block, :] = dot(part, values[i], ((0,), (0,))).astype(BF)
                pltpu.make_async_copy(
                    bufs[i].at[pl.ds(at, block)], outs[i].at[pl.ds(at, block)], sem.at[i]
                ).start()
        for i in range(n + combine):
            pltpu.make_async_copy(bufs[i], outs[i], sem.at[i]).wait()

    shapes = [(width, hidden)] * n + ([(pick_w.shape[1], width)] if combine else [])
    size = n * width * hidden * 2
    vmem = pl.BlockSpec(memory_space=pltpu.VMEM)
    operands = [rows, *cots] + ([pick_w, back] if combine else [])
    return pl.pallas_call(
        body,
        in_specs=[vmem] * len(operands),
        out_specs=[pl.BlockSpec(memory_space=pl.ANY)] * len(shapes),
        out_shape=[jax.ShapeDtypeStruct(shape, BF) for shape in shapes],
        scratch_shapes=[pltpu.VMEM(shape, BF) for shape in shapes]
        + [pltpu.SemaphoreType.DMA((len(shapes),))],
        compiler_params=pltpu.CompilerParams(vmem_limit_bytes=size + (10 << 20)),
        cost_estimate=pl.CostEstimate(flops=size * count, bytes_accessed=size, transcendentals=0),
    )(*operands)


def per_device(tokens, cotangent, expert_ids, gate_values, w_gate, w_up, w_down):
    devices = lax.axis_size("expert")
    span = devices // EXPERTS
    count, width = tokens.shape
    direct = devices <= 8
    even = lax.axis_index("dp") % 2 == 0
    me = lax.axis_index("expert")
    expert_ids, even, me = lax.optimization_barrier((expert_ids, even, me))

    steps = jnp.arange(devices, dtype=jnp.int32)
    labels = ((steps ^ me) if direct else steps) // span
    ids, gates = expert_ids.T, gate_values.T
    pick, pick_w, packed_x = route(labels, ids, gates, tokens, devices, direct)

    def move(blocks):
        if direct:
            return jnp.concatenate(exchange(blocks, "expert"), axis=0)
        rows = jnp.concatenate(blocks, axis=0) if len(blocks) > 1 else blocks[0]
        got = lax.all_to_all(rows.reshape(devices, CAP, -1), "expert", split_axis=0, concat_axis=0, tiled=True)
        return got.reshape(devices * CAP, -1)

    def cut(rows):
        return [rows[s * CAP:(s + 1) * CAP] for s in range(devices)] if direct else [rows]

    if direct:
        got = exchange(packed_x, "expert")
        rows = jnp.concatenate(got, axis=0)
    else:
        rows = move(packed_x)
    gate = core_sum(project(rows, w_gate), even)
    up = core_sum(project(rows, w_up), even)
    gate_swap, up_swap = first_swap(gate), first_swap(up)
    packed_g = pack_cotangent(pick_w, cotangent, up, devices, direct)
    packed_g = exchange(packed_g, "expert") if direct else [move(packed_g)]
    grads = jnp.concatenate(packed_g, axis=0)
    gate, up, grads = lax.optimization_barrier((gate, up, grads))
    hidden_grad = core_sum(project(grads, w_down), even)
    grad_swap = first_swap(hidden_grad)
    even_gate, even_up = shared_sum(gate, gate_swap), shared_sum(up, up_swap)
    gate = chip_sum(gate, gate_swap)
    up = chip_sum(up, up_swap)
    sigma = jax.nn.sigmoid(gate)
    active = gate * sigma
    hidden_h, gate, up, sigma, active, hidden_grad = lax.optimization_barrier(
        ((active * up).astype(BF), gate, up, sigma, active, hidden_grad))
    (hidden,) = join([hidden_h], even)
    part_out = dot(hidden, w_down, ((1,), (1,))).astype(BF)
    even_grad = shared_sum(hidden_grad, grad_swap)
    hidden_grad = chip_sum(hidden_grad, grad_swap)
    d_up = (hidden_grad * active).astype(BF)
    d_gate = (hidden_grad * up * sigma * (1.0 + gate * (1.0 - sigma))).astype(BF)
    (grad_down,) = weight_grads(grads, [hidden])
    part_out, d_up, d_gate, grad_down = lax.optimization_barrier((part_out, d_up, d_gate, grad_down))
    back_out = exchange(cut(part_out), "expert") if direct else [move(cut(part_out))]
    d_up, d_gate = join([d_up, d_gate], even)
    pair = lax.axis_size("dp") == 4
    if pair:
        product = even_grad * (even_gate * jax.nn.sigmoid(even_gate) * even_up)
    else:
        product = hidden_grad * hidden_h.astype(F32)
    score = jnp.sum(product, axis=1, keepdims=True)
    score = score + swap(score, "dp", 1)
    step = 2
    while not pair and step < lax.axis_size("dp"):
        score = 0.5 * (score + swap(score, "dp", step))
        step *= 2
    high = lax.reduce_precision(score, 8, 7)
    low = (score - high).astype(BF)
    high = high.astype(BF)
    lanes = jnp.arange(EXTRA)[None, :]
    extra = jnp.where(lanes < EXTRA // 2, high, low)
    part_in = (dot(d_gate, w_gate, ((1,), (1,))) + dot(d_up, w_up, ((1,), (1,)))).astype(BF)
    back_in = move(cut(jnp.concatenate([part_in, extra], axis=1)))

    late_w, back_out[0] = lax.optimization_barrier((pick_w, back_out[0], part_in))[:2]
    back_out = jnp.concatenate(back_out, axis=0)
    grad_gate, grad_up, output = weight_grads(rows, [d_gate, d_up], late_w, back_out)
    input_grad, gate_grad = finish(labels, ids, gates, pick, back_in)
    return output, input_grad, gate_grad.T, grad_gate, grad_up, grad_down


def solution(mesh):
    in_specs = (
        P(("groups", "expert"), "dp"),
        P(("groups", "expert"), "dp"),
        P(("groups", "expert"), None),
        P(("groups", "expert"), None),
        P("dp", "expert"),
        P("dp", "expert"),
        P("dp", "expert"),
    )
    out_specs = (
        P(("groups", "expert"), "dp"),
        P(("groups", "expert"), "dp"),
        P(("groups", "expert"), None),
        P(("groups", "dp"), "expert"),
        P(("groups", "dp"), "expert"),
        P(("groups", "dp"), "expert"),
    )
    return jax.shard_map(
        per_device, mesh=mesh, in_specs=in_specs, out_specs=out_specs, check_vma=False
    )
```
